32 devices in a mesh: groups: 2 (over y), tile: 4 (over z), segment: 2 (over core), mp: 2 (over x).
Axes of the slice: x: 2, y: 2, z: 4, core: 2. Of those that a mesh axis runs over, the one named last changes fastest.
Arguments:
- spectra: bfloat16 [2, 64, 48, 224], P(None, ('groups', 'tile')), parts along dimension 1, may hold values from -6 to 6
- valid: int32 [2, 64], P(None, 'groups'), parts along dimension 1, may hold values from 1 to 48, as said below
- project: bfloat16 [224, 16], replicated, may hold values from -0.375 to 0.375
- enc_in: bfloat16 [768, 3072], P(None, 'mp'), may hold values from -0.21875 to 0.21875
- enc_out: bfloat16 [3072, 768], P('mp'), may hold values from -0.109375 to 0.109375
- tok_embed: bfloat16 [48, 2048], replicated, may hold values from -0.875 to 0.875
- band_embed: bfloat16 [16, 2048], P('tile'), may hold values from -3 to 3
- dec_in: bfloat16 [2048, 8192], P('tile', 'mp'), may hold values from -0.125 to 0.125
- dec_out: bfloat16 [8192, 2048], P('mp', 'tile'), may hold values from -0.0625 to 0.0625
- head: bfloat16 [2048, 672], P('tile', 'mp'), may hold values from -0.125 to 0.125
Outputs:
- grad_project: float32 [448, 16], P(('groups', 'tile', 'segment')), parts along dimension 0
- grad_enc_in: float32 [1536, 3072], P(('groups', 'tile', 'segment'), 'mp'), parts along dimension 0
- grad_enc_out: float32 [6144, 768], P(('groups', 'mp'), ('tile', 'segment')), parts along dimension 0
The draws below stay inside these ranges and needn't reach their ends.
There are 2 independent parts, one for each index of `groups`. The reference program is written for one: setup_inputs(seed, part) draws one part's arguments, and reference() takes and returns one part's arrays. A program takes and returns all parts, laid end to end along the dimension named above; an argument that names none is the same for every part. Nothing has to cross between parts.
Inputs may be any that keep to these rules, and one draw needn't show every extreme that they name: Pixels of patch n in micro-batch m with index below valid[m, n] count in the loss.
All inputs are finite; a program needn't handle non-finite values.
Results may differ from the reference program's by a relative error of at most 0.018.
Values may be sent and summed in bfloat16 or wider, within the bound.
A program may use at most 128 MiB of HBM per device.

```python
import jax
import jax.numpy as jnp
from jax import lax

CB = 16
PP = 48
GB = 14
NB = 224
DS = 768
RO = 672
HS = 3072
DT = 2048
HT = 8192
MB = 2
NP = 32
SPLIT = 2


def draw_valid(key, part):
    counts = jax.random.randint(key, (MB, NP), 1, PP + 1)
    counts = counts.at[0, 0].set(PP)
    counts = counts.at[MB - 1, NP - 1].set(1)
    return counts.astype(jnp.int32)


def block_scale(rng, shape, pieces, low, top_value):
    loudness = 1.0
    for dim, parts in pieces:
        steps = jax.random.uniform(jax.random.fold_in(jax.random.fold_in(rng, 6), dim), (parts,), jnp.float32, low / len(pieces), top_value / len(pieces))
        loudness = loudness * jnp.repeat(jnp.exp(steps), shape[dim] // parts).reshape((-1,) + (1,) * (len(shape) - 1 - dim))
    return loudness


def gaussian(own_key, shape, scale, bound, split=(), kind=jnp.bfloat16):
    result = jax.random.normal(own_key, shape, jnp.float32) * scale
    if len(split) > 0:
        result = block_scale(own_key, shape, split, -0.22, 0.18) * result
    return jnp.clip(result, min=-bound, max=bound).astype(kind)


def setup_inputs(seed: int = 0, part: int = 0) -> dict:
    keys = jax.random.split(jax.random.key(seed), 11)
    part_keys = jax.random.split(jax.random.fold_in(keys[10], part), 11)
    return {
        "spectra": gaussian(part_keys[0], (MB, NP, PP, NB), 1.0, 6.0, ((1, 4),)),
        "valid": draw_valid(jax.random.fold_in(jax.random.fold_in(keys[10], part), 71), part),
        "project": gaussian(keys[2], (NB, CB), NB ** -0.5, 0.375),
        "enc_in": gaussian(keys[3], (DS, HS), DS ** -0.5, 0.21875, ((1, 2),)),
        "enc_out": gaussian(keys[4], (HS, DS), HS ** -0.5, 0.109375, ((0, 2),)),
        "tok_embed": gaussian(keys[5], (PP, DT), PP ** -0.5, 0.875),
        "band_embed": gaussian(keys[6], (CB, DT), 0.5, 3.0, ((0, 4),)),
        "dec_in": gaussian(keys[7], (DT, HT), DT ** -0.5, 0.125, ((0, 4), (1, 2))),
        "dec_out": gaussian(keys[8], (HT, DT), HT ** -0.5, 0.0625, ((0, 2), (1, 4))),
        "head": gaussian(keys[9], (DT, RO), DT ** -0.5, 0.125, ((0, 4), (1, 2))),
    }


def rms_norm(values):
    return values * lax.rsqrt(lax.optimization_barrier(jnp.mean(values * values, axis=-1, keepdims=True)) + 1e-05)

def rms_back(values, gradient):
    scaling = lax.rsqrt(lax.optimization_barrier(jnp.mean(values * values, axis=-1, keepdims=True)) + 1e-05)
    normed = values * scaling
    return scaling * (gradient - normed * lax.optimization_barrier(jnp.mean(gradient * normed, axis=-1, keepdims=True)))

def gelu_tanh(values):
    return jax.nn.gelu(values, approximate=True)

def gelu_back(pre_values, gradient):
    return jax.vjp(gelu_tanh, pre_values)[1](gradient)[0]

def block_sum(operand, factor, blocks):
    col_width = operand.shape[1] // blocks
    summed = jnp.zeros((operand.shape[0], factor.shape[1]), jnp.float32)
    for position in range(blocks):
        partial_value = jnp.dot(operand[:, position * col_width:(position + 1) * col_width], factor[position * col_width:(position + 1) * col_width], preferred_element_type=jnp.float32)
        rounded = lax.optimization_barrier(partial_value.astype(jnp.bfloat16))
        summed = summed + rounded.astype(jnp.float32)
    return summed

def reference(spectra, valid, project, enc_in, enc_out, tok_embed, band_embed, dec_in, dec_out, head):
    patch_count = spectra.shape[1]
    total_valid = jnp.sum(valid.astype(jnp.float32))
    loss_scale = 2.0 * MB * patch_count / total_valid
    pixel_index = jnp.arange(PP, dtype=jnp.int32)
    grad_project = jnp.zeros((NB, CB), jnp.float32)
    grad_enc_in = jnp.zeros((DS, HS), jnp.float32)
    grad_enc_out = jnp.zeros((HS, DS), jnp.float32)
    for microbatch in range(MB):
        pixels = spectra[microbatch].reshape(patch_count * PP, NB)
        band_codes = jnp.dot(pixels, project, preferred_element_type=jnp.float32).astype(jnp.bfloat16)
        features = band_codes.reshape(patch_count, PP, CB).transpose(0, 2, 1).reshape(patch_count, DS)
        normed = rms_norm(features.astype(jnp.float32)).astype(jnp.bfloat16)
        pre_act = jnp.dot(normed, enc_in, preferred_element_type=jnp.float32)
        act_out = gelu_tanh(pre_act).astype(jnp.bfloat16)
        encoded = (features.astype(jnp.float32) + block_sum(act_out, enc_out, SPLIT)).astype(jnp.bfloat16)
        band_tok = encoded.reshape(patch_count * CB, PP)
        band_rows = jnp.tile(band_embed.astype(jnp.float32), (patch_count, 1))
        embedded = (jnp.dot(band_tok, tok_embed, preferred_element_type=jnp.float32) + band_rows).astype(jnp.bfloat16)
        start_norm = rms_norm(embedded.astype(jnp.float32)).astype(jnp.bfloat16)
        hid_pre = jnp.dot(start_norm, dec_in, preferred_element_type=jnp.float32)
        hid_act = gelu_tanh(hid_pre).astype(jnp.bfloat16)
        decoded = (embedded.astype(jnp.float32) + block_sum(hid_act, dec_out, SPLIT)).astype(jnp.bfloat16)
        rebuilt = jnp.dot(decoded, head, preferred_element_type=jnp.float32)
        target = spectra[microbatch].reshape(patch_count, PP, CB, GB).transpose(0, 2, 1, 3).reshape(patch_count * CB, RO)
        valid_mask = (pixel_index[None, :] < valid[microbatch][:, None]).astype(jnp.float32)
        valid_mask = jnp.broadcast_to(valid_mask[:, None, :, None], (patch_count, CB, PP, GB)).reshape(patch_count * CB, RO)
        grad_rebuilt = (loss_scale * valid_mask * (rebuilt - target.astype(jnp.float32))).astype(jnp.bfloat16)
        grad_decoded = block_sum(grad_rebuilt, head.T, SPLIT)
        grad_hid = gelu_back(hid_pre, jnp.dot(grad_decoded.astype(jnp.bfloat16), dec_out.T, preferred_element_type=jnp.float32)).astype(jnp.bfloat16)
        grad_norm = block_sum(grad_hid, dec_in.T, SPLIT)
        grad_start = (grad_decoded + rms_back(embedded.astype(jnp.float32), grad_norm)).astype(jnp.bfloat16)
        grad_tok = jnp.dot(grad_start, tok_embed.T, preferred_element_type=jnp.float32).astype(jnp.bfloat16)
        grad_encoded = grad_tok.reshape(patch_count, DS)
        grad_act = gelu_back(pre_act, jnp.dot(grad_encoded, enc_out.T, preferred_element_type=jnp.float32)).astype(jnp.bfloat16)
        grad_normed = block_sum(grad_act, enc_in.T, SPLIT)
        grad_features = (grad_encoded.astype(jnp.float32) + rms_back(features.astype(jnp.float32), grad_normed)).astype(jnp.bfloat16)
        grad_codes = grad_features.reshape(patch_count, CB, PP).transpose(0, 2, 1).reshape(patch_count * PP, CB)
        grad_enc_out = grad_enc_out + jnp.dot(act_out.T, grad_encoded, preferred_element_type=jnp.float32)
        grad_enc_in = grad_enc_in + jnp.dot(normed.T, grad_act, preferred_element_type=jnp.float32)
        grad_project = grad_project + jnp.dot(pixels.T, grad_codes, preferred_element_type=jnp.float32)
    return (grad_project, grad_enc_in, grad_enc_out)
```

```python
import jax
import jax.numpy as jnp
from jax import lax
from jax.sharding import PartitionSpec as P

BF = jnp.bfloat16
F32 = jnp.float32


def inv_rms(values):
    return lax.rsqrt(jnp.mean(values * values, axis=-1, keepdims=True) + 1e-05)


def rms_back(values, gradient):
    scaling = inv_rms(values)
    normed = values * scaling
    return scaling * (gradient - normed * jnp.mean(gradient * normed, axis=-1, keepdims=True))


def gelu(v):
    return 0.5 * v * (1 + jnp.tanh(0.7978845608028654 * (v + 0.044715 * v * v * v)))


def gelu_and_slope(v):
    square = v * v
    t = jnp.tanh(0.7978845608028654 * v * (1 + 0.044715 * square))
    half = 0.5 * (1 + t)
    slope = half + 0.5 * v * (1 - t * t) * 0.7978845608028654 * (1 + 3 * 0.044715 * square)
    return v * half, slope


def dot(a, b):
    return jnp.dot(a, b, preferred_element_type=F32)


def dot_t(a, b):
    return lax.dot_general(a, b, (((1,), (1,)), ((), ())), preferred_element_type=F32)


def t_dot(a, b):
    return lax.dot_general(a, b, (((0,), (0,)), ((), ())), preferred_element_type=F32)


def body(spectra, valid, project, enc_in, enc_out, tok_embed, band_embed, dec_in, dec_out, head):
    tile, seg, mp = (lax.axis_index(a) for a in ("tile", "segment", "mp"))
    T, S, M = (lax.axis_size(a) for a in ("tile", "segment", "mp"))
    batches, per_tile, pixels, bands = spectra.shape
    codes = project.shape[1]
    width = bands // codes
    local = batches * per_tile
    share = local // (S * M)
    rows = T * local
    student = codes * pixels
    dim = tok_embed.shape[1]
    dt = dec_in.shape[0]
    hid = dec_in.shape[1] // S
    once = jnp.logical_and(seg == 0, mp == 0).astype(F32)

    patches = spectra.reshape(local, pixels, bands)
    flat = patches.reshape(local * pixels, bands)
    feat_local = (
        dot(flat, project).astype(BF).reshape(local, pixels, codes).transpose(0, 2, 1).reshape(local, student)
    )
    feats = lax.all_gather(feat_local, "tile")
    feats = feats.reshape(T, S, M, share, student).transpose(1, 2, 0, 3, 4).reshape(rows, student)
    band_all = lax.all_gather(band_embed, "tile", tiled=True)
    head_full = lax.all_gather(head, "mp", axis=1, tiled=True)

    embed = jnp.concatenate([tok_embed, band_all], axis=0)
    embed_z = lax.dynamic_slice_in_dim(embed, tile * dt, dt, 1)
    d_in = lax.dynamic_slice_in_dim(dec_in, seg * hid, hid, 1)
    d_out = lax.dynamic_slice_in_dim(dec_out, seg * hid, hid, 0)
    folded = lax.psum(dot(embed_z, d_in).astype(BF), "tile")
    fold_tok, fold_band = folded[:pixels], folded[pixels:]

    feats32 = feats.astype(F32)
    normed = (feats32 * inv_rms(feats32)).astype(BF)
    pre_act, pre_slope = gelu_and_slope(dot(normed, enc_in))
    act_out = pre_act.astype(BF)
    summed = lax.psum(dot(act_out, enc_out).astype(BF), "mp").astype(F32)
    encoded = (feats32 + summed).astype(BF)

    tokens = rows * codes
    tok = encoded.reshape(tokens, pixels)
    embedded = (
        dot(tok, tok_embed).reshape(rows, codes, dim) + band_all.astype(F32)
    ).reshape(tokens, dim).astype(BF)
    scaling = inv_rms(embedded.astype(F32))
    hid_pre = scaling * (
        dot(tok, fold_tok).reshape(rows, codes, hid) + fold_band.astype(F32)
    ).reshape(tokens, hid)
    hid_act, hid_slope = gelu_and_slope(hid_pre)
    embedded_z = lax.dynamic_slice_in_dim(embedded, tile * dt, dt, 1)
    decoded = (once * embedded_z.astype(F32) + dot(hid_act.astype(BF), d_out)).astype(BF)
    partial = dot(decoded, head_full).astype(BF)
    own = lax.psum_scatter(
        partial.reshape(S * M, T, share * codes, -1), ("segment", "mp"), scatter_dimension=0
    )
    own = lax.psum_scatter(own, "tile", scatter_dimension=0).astype(F32)
    quarter = (seg * M + mp) * share
    own_patches = lax.dynamic_slice_in_dim(patches, quarter, share, 0)
    target = (
        own_patches.reshape(share, pixels, codes, width).transpose(0, 2, 1, 3).reshape(share * codes, -1)
    )
    total_valid = jnp.sum(valid.astype(F32))
    loss_scale = 2.0 * batches * valid.shape[1] / total_valid
    own_valid = lax.dynamic_slice_in_dim(valid, tile * per_tile, per_tile, 1).reshape(local)
    own_valid = lax.dynamic_slice_in_dim(own_valid, quarter, share, 0)
    column = jnp.arange(pixels * width, dtype=jnp.int32) // width
    mask = (column[None, :] < jnp.repeat(own_valid, codes)[:, None]).astype(F32)
    grad_own = (loss_scale * mask * (own - target.astype(F32))).astype(BF)
    grad_rebuilt = lax.all_gather(
        lax.all_gather(grad_own, "tile"), ("segment", "mp")
    ).reshape(tokens, -1)

    grad_decoded = dot_t(grad_rebuilt, head_full).astype(BF)
    grad_hid = hid_slope * dot_t(grad_decoded, d_out)
    tok_z = lax.dynamic_slice_in_dim(tok_embed, tile * dt, dt, 1)
    unit_tok = dot_t((embedded.astype(F32) * scaling).astype(BF), tok_embed)
    along = jnp.sum(grad_hid * hid_pre, axis=1, keepdims=True) / dim
    grad_tok = scaling * (dot_t(grad_hid.astype(BF), fold_tok) - unit_tok * along)
    grad_tok = grad_tok + once * dot_t(grad_decoded, tok_z)
    grad_encoded = lax.psum(
        grad_tok.reshape(rows, student).astype(BF), ("tile", "segment", "mp")
    )

    grad_act = (pre_slope * dot_t(grad_encoded, enc_out)).astype(BF)
    columns = student // (T * S)
    start = (tile * S + seg) * columns
    grad_out = t_dot(act_out, lax.dynamic_slice_in_dim(grad_encoded, start, columns, 1))
    grad_in = t_dot(lax.dynamic_slice_in_dim(normed, start, columns, 1), grad_act)
    grad_normed = lax.psum(dot_t(grad_act, enc_in).astype(BF), "mp").astype(F32)
    own_rows = lambda a: lax.dynamic_slice_in_dim(
        a.reshape(S * M, T, share, student), tile, 1, 1
    ).reshape(local, student)
    grad_feat = (
        own_rows(grad_encoded).astype(F32) + rms_back(feat_local.astype(F32), own_rows(grad_normed))
    ).astype(BF)
    grad_codes = grad_feat.reshape(local, codes, pixels).transpose(0, 2, 1).reshape(-1, codes)
    grad_proj = jnp.sum(lax.all_gather(t_dot(flat, grad_codes), "tile"), axis=0)
    proj_rows = bands // (T * S)
    grad_proj = lax.dynamic_slice_in_dim(grad_proj, (tile * S + seg) * proj_rows, proj_rows, 0)
    return (grad_proj, grad_in, grad_out)


def solution(mesh):
    placed = (
        P(None, ("groups", "tile"), None, None),
        P(None, "groups"),
        P(),
        P(None, "mp"),
        P("mp", None),
        P(),
        P("tile", None),
        P("tile", "mp"),
        P("mp", "tile"),
        P("tile", "mp"),
    )
    return jax.shard_map(
        body,
        mesh=mesh,
        in_specs=placed,
        out_specs=(
            P(("groups", "tile", "segment"), None),
            P(("groups", "tile", "segment"), "mp"),
            P(("groups", "mp"), ("tile", "segment")),
        ),
        check_vma=False,
    )
```

```python
import jax
import jax.numpy as jnp
from jax import lax
from jax.experimental import pallas as pl
from jax.experimental.pallas import tpu as pltpu
from jax.sharding import PartitionSpec as P

BF = jnp.bfloat16
F32 = jnp.float32


def inv_rms(values):
    return lax.rsqrt(jnp.mean(values * values, axis=-1, keepdims=True) + 1e-05)


def rms_back(values, gradient):
    scaling = inv_rms(values)
    normed = values * scaling
    return scaling * (gradient - normed * jnp.mean(gradient * normed, axis=-1, keepdims=True))


def gelu(v):
    return 0.5 * v * (1 + jnp.tanh(0.7978845608028654 * (v + 0.044715 * v * v * v)))


def gelu_and_slope(v):
    square = v * v
    t = jnp.tanh(0.7978845608028654 * v * (1 + 0.044715 * square))
    half = 0.5 * (1 + t)
    slope = half + 0.5 * v * (1 - t * t) * 0.7978845608028654 * (1 + 3 * 0.044715 * square)
    return v * half, slope


def dot(a, b):
    return jnp.dot(a, b, preferred_element_type=F32)


def dot_t(a, b):
    return lax.dot_general(a, b, (((1,), (1,)), ((), ())), preferred_element_type=F32)


def t_dot(a, b):
    return lax.dot_general(a, b, (((0,), (0,)), ((), ())), preferred_element_type=F32)


MESH = pl.DeviceIdType.MESH
DMA = pltpu.SemaphoreType.DMA


def shifted(axis, step):
    return lax.rem(lax.axis_index(axis) + step, lax.axis_size(axis))


def greet(peers):
    barrier = pltpu.get_barrier_semaphore()
    for peer in peers:
        pl.semaphore_signal(barrier, inc=1, device_id=peer, device_id_type=MESH)
    pl.semaphore_wait(barrier, len(peers))


def ring(axis):
    return [{axis: shifted(axis, k)} for k in range(1, lax.axis_size(axis))]


def push(src, dst, send, recv, peer):
    copy = pltpu.make_async_remote_copy(
        src_ref=src, dst_ref=dst, send_sem=send, recv_sem=recv, device_id=peer, device_id_type=MESH
    )
    copy.start()
    return copy


def finish(copies):
    for copy in copies:
        copy.wait_recv()


def vmem_call(kernel, name, number, outs, scratch, *args):
    return pl.pallas_call(
        kernel,
        out_shape=outs,
        in_specs=[pl.BlockSpec(memory_space=pltpu.VMEM)] * len(args),
        out_specs=jax.tree.map(lambda _: pl.BlockSpec(memory_space=pltpu.VMEM), outs),
        scratch_shapes=scratch,
        compiler_params=pltpu.CompilerParams(
            collective_id=number, has_side_effects=True, vmem_limit_bytes=56 << 20
        ),
        name=name,
    )(*args)


def gather_tile(feat, band):
    count = lax.axis_size("tile")

    def kernel(feat_ref, band_ref, feats_ref, bands_ref, send, recv):
        me = lax.axis_index("tile")
        peers = ring("tile")
        greet(peers)
        copies = []
        for k, peer in enumerate(peers):
            copies.append(push(feat_ref, feats_ref.at[me], send.at[0, k], recv.at[0, k], peer))
            copies.append(push(band_ref, bands_ref.at[me], send.at[1, k], recv.at[1, k], peer))
        feats_ref[me] = feat_ref[...]
        bands_ref[me] = band_ref[...]
        for copy in copies:
            copy.wait()

    outs = [jax.ShapeDtypeStruct((count,) + a.shape, a.dtype) for a in (feat, band)]
    return vmem_call(kernel, "gather_tile", 0, outs, [DMA((2, count - 1))] * 2, feat, band)


def fold_exchange(fold, part, head):
    T, M = lax.axis_size("tile"), lax.axis_size("mp")

    def kernel(fold_ref, part_ref, head_ref, sum_ref, parts_ref, heads_ref, slots, send, recv, xsend, xrecv):
        me, mine = lax.axis_index("tile"), lax.axis_index("mp")
        tiles, mps = ring("tile"), ring("mp")
        greet(tiles + mps)
        first = []
        for k, peer in enumerate(tiles):
            first.append(push(fold_ref.at[peer["tile"]], slots.at[k], send.at[0, k], recv.at[0, k], peer))
        across = []
        for k, peer in enumerate(mps):
            across.append(push(part_ref, parts_ref.at[mine], xsend.at[0, k], xrecv.at[0, k], peer))
            across.append(push(head_ref, heads_ref.at[mine], xsend.at[1, k], xrecv.at[1, k], peer))
        parts_ref[mine] = part_ref[...]
        heads_ref[mine] = head_ref[...]
        finish(first)
        total = fold_ref[me].astype(F32)
        for k in range(T - 1):
            total = total + slots[k].astype(F32)
        sum_ref[me] = total.astype(BF)
        second = []
        for k, peer in enumerate(tiles):
            second.append(push(sum_ref.at[me], sum_ref.at[me], send.at[1, k], recv.at[1, k], peer))
        finish(second + across)
        for copy in first + second + across:
            copy.wait_send()

    outs = [
        jax.ShapeDtypeStruct(fold.shape, BF),
        jax.ShapeDtypeStruct((M,) + part.shape, BF),
        jax.ShapeDtypeStruct((M,) + head.shape, BF),
    ]
    scratch = [pltpu.VMEM((T - 1,) + fold.shape[1:], BF)] + [DMA((2, T - 1))] * 2 + [DMA((2, M - 1))] * 2
    return vmem_call(kernel, "fold_exchange", 1, outs, scratch, fold, part, head)


def rebuilt_exchange(part, target, factor):
    C, S, M, T, q, R = part.shape
    most = max(S, M, T) - 1

    def kernel(part_ref, target_ref, factor_ref, grad_ref, s_in, s_sum, m_in, m_sum, t_in, send, recv):
        s, m, t = (lax.axis_index(a) for a in ("segment", "mp", "tile"))
        segs, mps, tiles = ring("segment"), ring("mp"), ring("tile")
        greet(segs + mps + tiles)
        live = [None] * C
        everything = []

        def launch(c, stage, peers, source, landing):
            live[c] = [
                push(source(k, p), landing(k), send.at[stage, c, k], recv.at[stage, c, k], p)
                for k, p in enumerate(peers)
            ]
            everything.extend(live[c])

        def advance(c, stage):
            if stage > 0:
                finish(live[c])
            if stage == 0:
                launch(c, 0, segs, lambda k, p: part_ref.at[c, p["segment"]], lambda k: s_in.at[c, k])
            if stage == 1:
                for other in range(M):
                    total = part_ref[c, s, other].astype(F32)
                    for k in range(S - 1):
                        total = total + s_in[c, k, other].astype(F32)
                    s_sum[c, other] = total.astype(BF)
                launch(c, 1, mps, lambda k, p: s_sum.at[c, p["mp"]], lambda k: m_in.at[c, k])
            if stage == 2:
                total = s_sum[c, m].astype(F32)
                for k in range(M - 1):
                    total = total + m_in[c, k].astype(F32)
                m_sum[c] = total.astype(BF)
                launch(c, 2, tiles, lambda k, p: m_sum.at[c, p["tile"]], lambda k: t_in.at[c, k])
            if stage == 3:
                total = m_sum[c, t].astype(F32)
                for k in range(T - 1):
                    total = total + t_in[c, k].astype(F32)
                grad = factor_ref[c] * (total - target_ref[c].astype(F32))
                grad_ref[c, s, m, t] = grad.astype(BF)
                own = grad_ref.at[c, s, m, t]
                launch(c, 3, tiles, lambda k, p: own, lambda k: own)
            if stage == 4:
                own = grad_ref.at[c, s, m]
                launch(c, 4, mps, lambda k, p: own, lambda k: own)
            if stage == 5:
                own = grad_ref.at[c, s]
                launch(c, 5, segs, lambda k, p: own, lambda k: own)

        for step in range(7 + C - 1):
            for c in range(C):
                if 0 <= step - c <= 6:
                    advance(c, step - c)
        for copy in everything:
            copy.wait_send()

    scratch = [
        pltpu.VMEM((C, S - 1, M, T, q, R), BF),
        pltpu.VMEM((C, M, T, q, R), BF),
        pltpu.VMEM((C, M - 1, T, q, R), BF),
        pltpu.VMEM((C, T, q, R), BF),
        pltpu.VMEM((C, T - 1, q, R), BF),
        DMA((6, C, most)),
        DMA((6, C, most)),
    ]
    return vmem_call(
        kernel, "rebuilt_exchange", 2, jax.ShapeDtypeStruct(part.shape, BF), scratch, part, target, factor
    )


def token_sum(part):
    T, rows, width = part.shape
    S, M = lax.axis_size("segment"), lax.axis_size("mp")
    most = max(S, M, T) - 1

    def kernel(part_ref, sum_ref, s_in, s_sum, m_in, m_sum, t_in, send, recv):
        t = lax.axis_index("tile")
        segs, mps, tiles = ring("segment"), ring("mp"), ring("tile")
        greet(segs + mps + tiles)
        everything = []

        def launch(stage, peers, source, landing):
            copies = [
                push(source(p), landing(k), send.at[stage, k], recv.at[stage, k], p)
                for k, p in enumerate(peers)
            ]
            everything.extend(copies)
            finish(copies)

        launch(0, segs, lambda p: part_ref, lambda k: s_in.at[k])
        total = part_ref[...].astype(F32)
        for k in range(S - 1):
            total = total + s_in[k].astype(F32)
        s_sum[...] = total.astype(BF)
        launch(1, mps, lambda p: s_sum, lambda k: m_in.at[k])
        total = s_sum[...].astype(F32)
        for k in range(M - 1):
            total = total + m_in[k].astype(F32)
        m_sum[...] = total.astype(BF)
        launch(2, tiles, lambda p: m_sum.at[p["tile"]], lambda k: t_in.at[k])
        total = m_sum[t].astype(F32)
        for k in range(T - 1):
            total = total + t_in[k].astype(F32)
        sum_ref[t] = total.astype(BF)
        own = sum_ref.at[t]
        launch(3, tiles, lambda p: own, lambda k: own)
        for copy in everything:
            copy.wait_send()

    scratch = [
        pltpu.VMEM((S - 1,) + part.shape, BF),
        pltpu.VMEM(part.shape, BF),
        pltpu.VMEM((M - 1,) + part.shape, BF),
        pltpu.VMEM(part.shape, BF),
        pltpu.VMEM((T - 1, rows, width), BF),
        DMA((4, most)),
        DMA((4, most)),
    ]
    return vmem_call(kernel, "token_sum", 3, jax.ShapeDtypeStruct(part.shape, BF), scratch, part)


def project_sum(part):
    T, S, M = (lax.axis_size(a) for a in ("tile", "segment", "mp"))
    count = T * M

    def kernel(part_ref, sum_ref, slots, send, recv):
        s, t = lax.axis_index("segment"), lax.axis_index("tile")
        peers = [
            {"tile": shifted("tile", k // M), "mp": shifted("mp", k % M)} for k in range(1, count)
        ]
        greet(peers)
        copies = []
        for k, peer in enumerate(peers):
            copies.append(
                push(part_ref.at[peer["tile"] * S + s], slots.at[k], send.at[k], recv.at[k], peer)
            )
        finish(copies)
        total = part_ref[t * S + s]
        for k in range(count - 1):
            total = total + slots[k]
        sum_ref[...] = total
        for copy in copies:
            copy.wait_send()

    scratch = [pltpu.VMEM((count - 1,) + part.shape[1:], F32), DMA((count - 1,)), DMA((count - 1,))]
    return vmem_call(kernel, "project_sum", 4, jax.ShapeDtypeStruct(part.shape[1:], F32), scratch, part)


def body(spectra, valid, project, enc_in, enc_out, tok_embed, band_embed, dec_in, dec_out, head):
    tile, seg, mp = (lax.axis_index(a) for a in ("tile", "segment", "mp"))
    T, S, M = (lax.axis_size(a) for a in ("tile", "segment", "mp"))
    batches, per_tile, pixels, bands = spectra.shape
    codes = project.shape[1]
    width = bands // codes
    local = batches * per_tile
    share = local // (S * M)
    parts = 2 if share % 2 == 0 else 1
    piece = share // parts
    rows = T * local
    student = codes * pixels
    dim = tok_embed.shape[1]
    dt = dec_in.shape[0]
    hid = dec_in.shape[1] // S
    once = jnp.logical_and(seg == 0, mp == 0).astype(F32)

    patches = spectra.reshape(local, pixels, bands)
    flat = patches.reshape(local * pixels, bands)
    feat_local = (
        dot(flat, project).astype(BF).reshape(local, pixels, codes).transpose(0, 2, 1).reshape(local, student)
    )
    feats, band_all = gather_tile(feat_local, band_embed)
    feats = (
        feats.reshape(T, parts, S, M, piece, student).transpose(1, 2, 3, 0, 4, 5).reshape(rows, student)
    )
    band_all = band_all.reshape(codes, dim)

    embed = jnp.concatenate([tok_embed, band_all], axis=0)
    embed_z = lax.dynamic_slice_in_dim(embed, tile * dt, dt, 1)
    d_in = lax.dynamic_slice_in_dim(dec_in, seg * hid, hid, 1)
    d_out = lax.dynamic_slice_in_dim(dec_out, seg * hid, hid, 0)
    fold_part = dot(embed_z, d_in).astype(BF).reshape(-1, T, hid // T).transpose(1, 0, 2)

    feats32 = feats.astype(F32)
    normed = (feats32 * inv_rms(feats32)).astype(BF)
    pre_act, pre_slope = gelu_and_slope(dot(normed, enc_in))
    act_out = pre_act.astype(BF)
    folded, summed, heads = fold_exchange(fold_part, dot(act_out, enc_out).astype(BF), head)
    folded = folded.transpose(1, 0, 2).reshape(-1, hid)
    fold_tok, fold_band = folded[:pixels], folded[pixels:]
    head_full = heads.transpose(1, 0, 2).reshape(dt, -1)
    summed = jnp.sum(summed.astype(F32), axis=0)
    encoded = (feats32 + summed).astype(BF)

    tokens = rows * codes
    tok = encoded.reshape(tokens, pixels)
    embedded = (
        dot(tok, tok_embed).reshape(rows, codes, dim) + band_all.astype(F32)
    ).reshape(tokens, dim).astype(BF)
    scaling = inv_rms(embedded.astype(F32))
    hid_pre = scaling * (
        dot(tok, fold_tok).reshape(rows, codes, hid) + fold_band.astype(F32)
    ).reshape(tokens, hid)
    hid_act, hid_slope = gelu_and_slope(hid_pre)
    embedded_z = lax.dynamic_slice_in_dim(embedded, tile * dt, dt, 1)
    decoded = (once * embedded_z.astype(F32) + dot(hid_act.astype(BF), d_out)).astype(BF)
    partial = dot(decoded, head_full).astype(BF)
    place = (seg * M + mp) * piece

    def mine(a):
        a = a.reshape((parts, S * M * piece) + a.shape[1:])
        a = lax.dynamic_slice_in_dim(a, place, piece, 1)
        return a.reshape((share,) + a.shape[2:])

    own_patches = mine(patches)
    target = (
        own_patches.reshape(share, pixels, codes, width).transpose(0, 2, 1, 3).reshape(share * codes, -1)
    )
    total_valid = jnp.sum(valid.astype(F32))
    loss_scale = 2.0 * batches * valid.shape[1] / total_valid
    own_valid = lax.dynamic_slice_in_dim(valid, tile * per_tile, per_tile, 1).reshape(local)
    own_valid = mine(own_valid)
    column = jnp.arange(pixels * width, dtype=jnp.int32) // width
    mask = (column[None, :] < jnp.repeat(own_valid, codes)[:, None]).astype(F32)
    block = (parts, piece * codes, pixels * width)
    grad_rebuilt = rebuilt_exchange(
        partial.reshape(parts, S, M, T, piece * codes, -1),
        target.reshape(block),
        (loss_scale * mask).reshape(block),
    ).reshape(tokens, -1)

    grad_decoded = dot_t(grad_rebuilt, head_full).astype(BF)
    grad_hid = hid_slope * dot_t(grad_decoded, d_out)
    tok_z = lax.dynamic_slice_in_dim(tok_embed, tile * dt, dt, 1)
    unit_tok = dot_t((embedded.astype(F32) * scaling).astype(BF), tok_embed)
    along = jnp.sum(grad_hid * hid_pre, axis=1, keepdims=True) / dim
    grad_tok = scaling * (dot_t(grad_hid.astype(BF), fold_tok) - unit_tok * along)
    grad_tok = grad_tok + once * dot_t(grad_decoded, tok_z)
    grad_encoded = token_sum(grad_tok.reshape(T, local, student).astype(BF)).reshape(rows, student)

    grad_act = (pre_slope * dot_t(grad_encoded, enc_out)).astype(BF)
    columns = student // (T * S)
    start = (tile * S + seg) * columns
    grad_out = t_dot(act_out, lax.dynamic_slice_in_dim(grad_encoded, start, columns, 1))
    grad_in = t_dot(lax.dynamic_slice_in_dim(normed, start, columns, 1), grad_act)
    own_rows = lambda a: lax.dynamic_slice_in_dim(
        a.reshape(parts * S * M, T, piece, student), tile, 1, 1
    ).reshape(local, student)
    grad_normed = own_rows(dot_t(grad_act, enc_in).astype(BF)).astype(F32)
    grad_feat = (
        jnp.where(mp == 0, own_rows(grad_encoded).astype(F32), 0.0)
        + rms_back(feat_local.astype(F32), grad_normed)
    ).astype(BF)
    grad_codes = grad_feat.reshape(local, codes, pixels).transpose(0, 2, 1).reshape(-1, codes)
    grad_proj = project_sum(t_dot(flat, grad_codes).reshape(T * S, -1, codes))
    return (grad_proj, grad_in, grad_out)


def solution(mesh):
    placed = (
        P(None, ("groups", "tile"), None, None),
        P(None, "groups"),
        P(),
        P(None, "mp"),
        P("mp", None),
        P(),
        P("tile", None),
        P("tile", "mp"),
        P("mp", "tile"),
        P("tile", "mp"),
    )
    return jax.shard_map(
        body,
        mesh=mesh,
        in_specs=placed,
        out_specs=(
            P(("groups", "tile", "segment"), None),
            P(("groups", "tile", "segment"), "mp"),
            P(("groups", "mp"), ("tile", "segment")),
        ),
        check_vma=False,
    )
```

```python
import jax
import jax.numpy as jnp
from jax import lax
from jax.experimental import pallas as pl
from jax.experimental.pallas import tpu as pltpu
from jax.sharding import PartitionSpec as P

BF = jnp.bfloat16
F32 = jnp.float32


def inv_rms(values):
    return lax.rsqrt(jnp.mean(values * values, axis=-1, keepdims=True) + 1e-05)


def rms_back(values, gradient):
    scaling = inv_rms(values)
    normed = values * scaling
    return scaling * (gradient - normed * jnp.mean(gradient * normed, axis=-1, keepdims=True))


def gelu(v):
    return 0.5 * v * (1 + jnp.tanh(0.7978845608028654 * (v + 0.044715 * v * v * v)))


def gelu_and_slope(v):
    square = v * v
    t = jnp.tanh(0.7978845608028654 * v * (1 + 0.044715 * square))
    half = 0.5 * (1 + t)
    slope = half + 0.5 * v * (1 - t * t) * 0.7978845608028654 * (1 + 3 * 0.044715 * square)
    return v * half, slope


def dot(a, b):
    return jnp.dot(a, b, preferred_element_type=F32)


def dot_t(a, b):
    return lax.dot_general(a, b, (((1,), (1,)), ((), ())), preferred_element_type=F32)


def t_dot(a, b):
    return lax.dot_general(a, b, (((0,), (0,)), ((), ())), preferred_element_type=F32)


MESH = pl.DeviceIdType.MESH
DMA = pltpu.SemaphoreType.DMA


def shifted(axis, step):
    return lax.rem(lax.axis_index(axis) + step, lax.axis_size(axis))


def greet(peers):
    barrier = pltpu.get_barrier_semaphore()
    for peer in peers:
        pl.semaphore_signal(barrier, inc=1, device_id=peer, device_id_type=MESH)
    pl.semaphore_wait(barrier, len(peers))


def ring(axis):
    return [{axis: shifted(axis, k)} for k in range(1, lax.axis_size(axis))]


def push(src, dst, send, recv, peer):
    copy = pltpu.make_async_remote_copy(
        src_ref=src, dst_ref=dst, send_sem=send, recv_sem=recv, device_id=peer, device_id_type=MESH
    )
    copy.start()
    return copy


def finish(copies):
    for copy in copies:
        copy.wait_recv()


def vmem_call(kernel, name, number, outs, scratch, *args):
    return pl.pallas_call(
        kernel,
        out_shape=outs,
        in_specs=[pl.BlockSpec(memory_space=pltpu.VMEM)] * len(args),
        out_specs=jax.tree.map(lambda _: pl.BlockSpec(memory_space=pltpu.VMEM), outs),
        scratch_shapes=scratch,
        compiler_params=pltpu.CompilerParams(
            collective_id=number, has_side_effects=True, vmem_limit_bytes=56 << 20
        ),
        name=name,
    )(*args)


def gather_tile(feat, band):
    count = lax.axis_size("tile")

    def kernel(feat_ref, band_ref, feats_ref, bands_ref, send, recv):
        me = lax.axis_index("tile")
        peers = ring("tile")
        greet(peers)
        copies = []
        for k, peer in enumerate(peers):
            copies.append(push(feat_ref, feats_ref.at[me], send.at[0, k], recv.at[0, k], peer))
            copies.append(push(band_ref, bands_ref.at[me], send.at[1, k], recv.at[1, k], peer))
        feats_ref[me] = feat_ref[...]
        bands_ref[me] = band_ref[...]
        for copy in copies:
            copy.wait()

    outs = [jax.ShapeDtypeStruct((count,) + a.shape, a.dtype) for a in (feat, band)]
    return vmem_call(kernel, "gather_tile", 0, outs, [DMA((2, count - 1))] * 2, feat, band)


def fold_exchange(fold, part, head):
    T, M = lax.axis_size("tile"), lax.axis_size("mp")

    def kernel(fold_ref, part_ref, head_ref, sum_ref, parts_ref, heads_ref, slots, send, recv, xsend, xrecv):
        me, mine = lax.axis_index("tile"), lax.axis_index("mp")
        tiles, mps = ring("tile"), ring("mp")
        greet(tiles + mps)
        first = []
        for k, peer in enumerate(tiles):
            first.append(push(fold_ref.at[peer["tile"]], slots.at[k], send.at[0, k], recv.at[0, k], peer))
        across = []
        for k, peer in enumerate(mps):
            across.append(push(part_ref, parts_ref.at[mine], xsend.at[0, k], xrecv.at[0, k], peer))
            across.append(push(head_ref, heads_ref.at[mine], xsend.at[1, k], xrecv.at[1, k], peer))
        parts_ref[mine] = part_ref[...]
        heads_ref[mine] = head_ref[...]
        finish(first)
        total = fold_ref[me].astype(F32)
        for k in range(T - 1):
            total = total + slots[k].astype(F32)
        sum_ref[me] = total.astype(BF)
        second = []
        for k, peer in enumerate(tiles):
            second.append(push(sum_ref.at[me], sum_ref.at[me], send.at[1, k], recv.at[1, k], peer))
        finish(second + across)
        for copy in first + second + across:
            copy.wait_send()

    outs = [
        jax.ShapeDtypeStruct(fold.shape, BF),
        jax.ShapeDtypeStruct((M,) + part.shape, BF),
        jax.ShapeDtypeStruct((M,) + head.shape, BF),
    ]
    scratch = [pltpu.VMEM((T - 1,) + fold.shape[1:], BF)] + [DMA((2, T - 1))] * 2 + [DMA((2, M - 1))] * 2
    return vmem_call(kernel, "fold_exchange", 1, outs, scratch, fold, part, head)


def teacher(x64, embed, folded, d_out, headt, target, factor, pixels):
    S, M, T = (lax.axis_size(a) for a in ("segment", "mp", "tile"))
    C, q, R = target.shape
    owners = S * M * T
    group = min(owners, 256 // q)
    rows = group * q
    blocks = owners // group
    K = x64.shape[1]
    dim = embed.shape[1]
    dt = d_out.shape[1]
    slabs, _, slab = folded.shape
    hid = slabs * slab
    step_cols = min(512, dim)
    most = max(S, M, T) - 1

    def kernel(
        x_ref, embed_ref, fold_ref, dout_hbm, head_ref, target_ref, factor_ref, out_ref,
        dout, pre_ref, slope_ref, scale_ref, unit_ref,
        part_ref, grad_ref, s_in, s_sum, m_in, m_sum, t_in, send, recv, load,
    ):
        s, m, t = (lax.axis_index(a) for a in ("segment", "mp", "tile"))
        segs, mps, tiles = ring("segment"), ring("mp"), ring("tile")
        fetch = pltpu.make_async_copy(dout_hbm.at[pl.ds(s * hid, hid)], dout, load)
        fetch.start()
        once = jnp.logical_and(s == 0, m == 0).astype(F32)
        own_cols = pl.ds(pl.multiple_of(t * dt, dt), dt)

        def scales(c, i):
            x = x_ref[c, pl.ds(i * rows, rows), :]
            total = jnp.zeros((rows, 1), F32)
            unit = jnp.zeros((rows, pixels), F32)
            for b in range(dim // step_cols):
                cols = slice(b * step_cols, (b + 1) * step_cols)
                e = dot(x, embed_ref[:, cols]).astype(BF)
                e32 = e.astype(F32)
                total = total + jnp.sum(e32 * e32, axis=1, keepdims=True)
                unit = unit + dot_t(e, embed_ref[:pixels, cols])
            scale = lax.rsqrt(total / dim + 1e-05)
            scale_ref[c, i] = scale
            unit_ref[c, i] = unit * scale

        def forward(c, i):
            scales(c, i)
            x = x_ref[c, pl.ds(i * rows, rows), :]
            scale = scale_ref[c, i]

            def hidden(h, acc):
                pre = scale * dot(x, fold_ref[h])
                act, slope = gelu_and_slope(pre)
                pre_ref[c, i, h] = pre
                slope_ref[c, i, h] = slope
                return acc + dot(act.astype(BF), dout[pl.ds(pl.multiple_of(h * slab, slab), slab), :])

            start = once * dot(x, embed_ref[:, own_cols]).astype(BF).astype(F32)
            acc = lax.fori_loop(0, slabs, hidden, start)
            part = dot_t(acc.astype(BF), head_ref[...]).astype(BF)
            part_ref[c, pl.ds(i * group, group)] = part.reshape(group, q, R)

        def backward(c, i):
            grad = grad_ref[c, pl.ds(i * group, group)].reshape(rows, R)
            gd = dot(grad, head_ref[...]).astype(BF)
            direct = once * dot_t(gd, embed_ref[:pixels, own_cols])

            def hidden(h, carry):
                acc, along = carry
                back = dot_t(gd, dout[pl.ds(pl.multiple_of(h * slab, slab), slab), :])
                gh = slope_ref[c, i, h] * back
                along = along + jnp.sum(gh * pre_ref[c, i, h], axis=1, keepdims=True)
                return acc + dot_t(gh.astype(BF), fold_ref[h, :pixels, :]), along

            acc, along = lax.fori_loop(
                0, slabs, hidden, (jnp.zeros((rows, pixels), F32), jnp.zeros((rows, 1), F32))
            )
            result = scale_ref[c, i] * (acc - unit_ref[c, i] * (along / dim)) + direct
            out_ref[c, pl.ds(i * rows, rows), :] = result.astype(BF)

        def over(function, c):
            if blocks == 1:
                function(c, 0)
            else:
                lax.fori_loop(0, blocks, lambda i, _: (function(c, i), 0)[1], 0)

        live = [None] * C
        everything = []

        def launch(c, stage, peers, source, landing):
            live[c] = [
                push(source(k, p), landing(k), send.at[stage, c, k], recv.at[stage, c, k], p)
                for k, p in enumerate(peers)
            ]
            everything.extend(live[c])

        def advance(c, stage):
            if stage > 0:
                finish(live[c])
            if stage == 0:
                launch(c, 0, segs, lambda k, p: part_ref.at[c, pl.ds(p["segment"] * M * T, M * T)], lambda k: s_in.at[c, k])
            if stage == 1:
                total = part_ref[c, pl.ds(s * M * T, M * T)].astype(F32)
                for k in range(S - 1):
                    total = total + s_in[c, k].astype(F32)
                s_sum[c] = total.astype(BF)
                launch(c, 1, mps, lambda k, p: s_sum.at[c, pl.ds(p["mp"] * T, T)], lambda k: m_in.at[c, k])
            if stage == 2:
                total = s_sum[c, pl.ds(m * T, T)].astype(F32)
                for k in range(M - 1):
                    total = total + m_in[c, k].astype(F32)
                m_sum[c] = total.astype(BF)
                launch(c, 2, tiles, lambda k, p: m_sum.at[c, p["tile"]], lambda k: t_in.at[c, k])
            if stage == 3:
                total = m_sum[c, t].astype(F32)
                for k in range(T - 1):
                    total = total + t_in[c, k].astype(F32)
                grad = factor_ref[c] * (total - target_ref[c].astype(F32))
                place = (s * M + m) * T + t
                grad_ref[c, place] = grad.astype(BF)
                own = grad_ref.at[c, place]
                launch(c, 3, tiles, lambda k, p: own, lambda k: own)
            if stage == 4:
                own = grad_ref.at[c, pl.ds((s * M + m) * T, T)]
                launch(c, 4, mps, lambda k, p: own, lambda k: own)
            if stage == 5:
                own = grad_ref.at[c, pl.ds(s * M * T, M * T)]
                launch(c, 5, segs, lambda k, p: own, lambda k: own)

        greet(segs + mps + tiles)
        fetch.wait()
        for step in range(7 + C):
            for c in range(C):
                stage = step - c - 1
                if 0 <= stage <= 6:
                    advance(c, stage)
            for c in range(C):
                if step == c:
                    over(forward, c)
                if step - c - 1 == 6:
                    over(backward, c)
        for copy in everything:
            copy.wait_send()

    vm = pltpu.VMEM
    scratch = [
        vm((hid, dt), BF),
        vm((C, blocks, slabs, rows, slab), F32),
        vm((C, blocks, slabs, rows, slab), F32),
        vm((C, blocks, rows, 1), F32),
        vm((C, blocks, rows, pixels), F32),
        vm((C, owners, q, R), BF),
        vm((C, owners, q, R), BF),
        vm((C, S - 1, M * T, q, R), BF),
        vm((C, M * T, q, R), BF),
        vm((C, M - 1, T, q, R), BF),
        vm((C, T, q, R), BF),
        vm((C, T - 1, q, R), BF),
        DMA((6, C, most)),
        DMA((6, C, most)),
        DMA,
    ]
    whole = pl.BlockSpec(memory_space=pltpu.VMEM)
    return pl.pallas_call(
        kernel,
        out_shape=jax.ShapeDtypeStruct((C, owners * q, pixels), BF),
        in_specs=[whole] * 3 + [pl.BlockSpec(memory_space=pl.ANY)] + [whole] * 3,
        out_specs=whole,
        scratch_shapes=scratch,
        compiler_params=pltpu.CompilerParams(
            collective_id=2, has_side_effects=True, vmem_limit_bytes=56 << 20
        ),
        name="teacher",
    )(x64.reshape(C, owners * q, K), embed, folded, d_out, headt, target, factor)


def token_sum(part):
    T, rows, width = part.shape
    S, M = lax.axis_size("segment"), lax.axis_size("mp")
    most = max(S, M, T) - 1

    def kernel(part_ref, sum_ref, s_in, s_sum, m_in, m_sum, t_in, send, recv):
        t = lax.axis_index("tile")
        segs, mps, tiles = ring("segment"), ring("mp"), ring("tile")
        greet(segs + mps + tiles)
        everything = []

        def launch(stage, peers, source, landing):
            copies = [
                push(source(p), landing(k), send.at[stage, k], recv.at[stage, k], p)
                for k, p in enumerate(peers)
            ]
            everything.extend(copies)
            finish(copies)

        launch(0, segs, lambda p: part_ref, lambda k: s_in.at[k])
        total = part_ref[...].astype(F32)
        for k in range(S - 1):
            total = total + s_in[k].astype(F32)
        s_sum[...] = total.astype(BF)
        launch(1, mps, lambda p: s_sum, lambda k: m_in.at[k])
        total = s_sum[...].astype(F32)
        for k in range(M - 1):
            total = total + m_in[k].astype(F32)
        m_sum[...] = total.astype(BF)
        launch(2, tiles, lambda p: m_sum.at[p["tile"]], lambda k: t_in.at[k])
        total = m_sum[t].astype(F32)
        for k in range(T - 1):
            total = total + t_in[k].astype(F32)
        sum_ref[t] = total.astype(BF)
        own = sum_ref.at[t]
        launch(3, tiles, lambda p: own, lambda k: own)
        for copy in everything:
            copy.wait_send()

    scratch = [
        pltpu.VMEM((S - 1,) + part.shape, BF),
        pltpu.VMEM(part.shape, BF),
        pltpu.VMEM((M - 1,) + part.shape, BF),
        pltpu.VMEM(part.shape, BF),
        pltpu.VMEM((T - 1, rows, width), BF),
        DMA((4, most)),
        DMA((4, most)),
    ]
    return vmem_call(kernel, "token_sum", 3, jax.ShapeDtypeStruct(part.shape, BF), scratch, part)


def project_sum(part):
    T, S, M = (lax.axis_size(a) for a in ("tile", "segment", "mp"))
    count = T * M

    def kernel(part_ref, sum_ref, slots, send, recv):
        s, t = lax.axis_index("segment"), lax.axis_index("tile")
        peers = [
            {"tile": shifted("tile", k // M), "mp": shifted("mp", k % M)} for k in range(1, count)
        ]
        greet(peers)
        copies = []
        for k, peer in enumerate(peers):
            copies.append(
                push(part_ref.at[peer["tile"] * S + s], slots.at[k], send.at[k], recv.at[k], peer)
            )
        finish(copies)
        total = part_ref[t * S + s]
        for k in range(count - 1):
            total = total + slots[k]
        sum_ref[...] = total
        for copy in copies:
            copy.wait_send()

    scratch = [pltpu.VMEM((count - 1,) + part.shape[1:], F32), DMA((count - 1,)), DMA((count - 1,))]
    return vmem_call(kernel, "project_sum", 4, jax.ShapeDtypeStruct(part.shape[1:], F32), scratch, part)


def body(spectra, valid, project, enc_in, enc_out, tok_embed, band_embed, dec_in, dec_out, head):
    tile, seg, mp = (lax.axis_index(a) for a in ("tile", "segment", "mp"))
    T, S, M = (lax.axis_size(a) for a in ("tile", "segment", "mp"))
    batches, per_tile, pixels, bands = spectra.shape
    codes = project.shape[1]
    width = bands // codes
    local = batches * per_tile
    share = local // (S * M)
    parts = 2 if share % 2 == 0 else 1
    piece = share // parts
    rows = T * local
    student = codes * pixels
    dim = tok_embed.shape[1]
    dt = dec_in.shape[0]
    hid = dec_in.shape[1] // S

    patches = spectra.reshape(local, pixels, bands)
    flat = patches.reshape(local * pixels, bands)
    feat_local = (
        dot(flat, project).astype(BF).reshape(local, pixels, codes).transpose(0, 2, 1).reshape(local, student)
    )
    feats, band_all = gather_tile(feat_local, band_embed)
    feats = (
        feats.reshape(T, parts, S, M, piece, student).transpose(1, 2, 3, 0, 4, 5).reshape(rows, student)
    )
    band_all = band_all.reshape(codes, dim)

    embed = jnp.concatenate([tok_embed, band_all], axis=0)
    embed_z = lax.dynamic_slice_in_dim(embed, tile * dt, dt, 1)
    d_in = lax.dynamic_slice_in_dim(dec_in, seg * hid, hid, 1)
    fold_part = dot(embed_z, d_in).astype(BF).reshape(-1, T, hid // T).transpose(1, 0, 2)

    feats32 = feats.astype(F32)
    normed = (feats32 * inv_rms(feats32)).astype(BF)
    pre_act, pre_slope = gelu_and_slope(dot(normed, enc_in))
    act_out = pre_act.astype(BF)
    folded, summed, heads = fold_exchange(fold_part, dot(act_out, enc_out).astype(BF), head.T)
    headt = heads.reshape(-1, dt)
    if hid // T < 128:
        folded = folded.transpose(1, 0, 2).reshape(1, -1, hid)
    summed = jnp.sum(summed.astype(F32), axis=0)
    encoded = (feats32 + summed).astype(BF)

    tokens = rows * codes
    tok = encoded.reshape(tokens, pixels)
    which = jnp.broadcast_to(jnp.eye(codes, dtype=BF), (rows, codes, codes)).reshape(tokens, codes)
    x64 = jnp.concatenate([tok, which], axis=1)
    place = (seg * M + mp) * piece

    def mine(a):
        a = a.reshape((parts, S * M * piece) + a.shape[1:])
        a = lax.dynamic_slice_in_dim(a, place, piece, 1)
        return a.reshape((share,) + a.shape[2:])

    own_patches = mine(patches)
    target = (
        own_patches.reshape(share, pixels, codes, width).transpose(0, 2, 1, 3).reshape(share * codes, -1)
    )
    total_valid = jnp.sum(valid.astype(F32))
    loss_scale = 2.0 * batches * valid.shape[1] / total_valid
    own_valid = lax.dynamic_slice_in_dim(valid, tile * per_tile, per_tile, 1).reshape(local)
    own_valid = mine(own_valid)
    column = jnp.arange(pixels * width, dtype=jnp.int32) // width
    mask = (column[None, :] < jnp.repeat(own_valid, codes)[:, None]).astype(F32)
    block = (parts, piece * codes, pixels * width)
    grad_tok = teacher(
        x64,
        embed,
        folded,
        dec_out,
        headt,
        target.reshape(block),
        (loss_scale * mask).reshape(block),
        pixels,
    )
    grad_encoded = token_sum(grad_tok.reshape(T, local, student)).reshape(rows, student)

    grad_act = (pre_slope * dot_t(grad_encoded, enc_out)).astype(BF)
    columns = student // (T * S)
    start = (tile * S + seg) * columns
    grad_out = t_dot(act_out, lax.dynamic_slice_in_dim(grad_encoded, start, columns, 1))
    grad_in = t_dot(lax.dynamic_slice_in_dim(normed, start, columns, 1), grad_act)
    own_rows = lambda a: lax.dynamic_slice_in_dim(
        a.reshape(parts * S * M, T, piece, student), tile, 1, 1
    ).reshape(local, student)
    grad_normed = own_rows(dot_t(grad_act, enc_in).astype(BF)).astype(F32)
    grad_feat = (
        jnp.where(mp == 0, own_rows(grad_encoded).astype(F32), 0.0)
        + rms_back(feat_local.astype(F32), grad_normed)
    ).astype(BF)
    grad_codes = grad_feat.reshape(local, codes, pixels).transpose(0, 2, 1).reshape(-1, codes)
    grad_proj = project_sum(t_dot(flat, grad_codes).reshape(T * S, -1, codes))
    return (grad_proj, grad_in, grad_out)


def solution(mesh):
    placed = (
        P(None, ("groups", "tile"), None, None),
        P(None, "groups"),
        P(),
        P(None, "mp"),
        P("mp", None),
        P(),
        P("tile", None),
        P("tile", "mp"),
        P("mp", "tile"),
        P("tile", "mp"),
    )
    return jax.shard_map(
        body,
        mesh=mesh,
        in_specs=placed,
        out_specs=(
            P(("groups", "tile", "segment"), None),
            P(("groups", "tile", "segment"), "mp"),
            P(("groups", "mp"), ("tile", "segment")),
        ),
        check_vma=False,
    )
```

```python
import jax
import jax.numpy as jnp
from jax import lax
from jax.experimental import pallas as pl
from jax.experimental.pallas import tpu as pltpu
from jax.sharding import PartitionSpec as P

BF = jnp.bfloat16
F32 = jnp.float32


def inv_rms(values):
    return lax.rsqrt(jnp.mean(values * values, axis=-1, keepdims=True) + 1e-05)


def rms_back(values, gradient):
    scaling = inv_rms(values)
    normed = values * scaling
    return scaling * (gradient - normed * jnp.mean(gradient * normed, axis=-1, keepdims=True))


def gelu(v):
    return 0.5 * v * (1 + jnp.tanh(0.7978845608028654 * (v + 0.044715 * v * v * v)))


def gelu_and_slope(v):
    square = v * v
    t = jnp.tanh(0.7978845608028654 * v * (1 + 0.044715 * square))
    half = 0.5 * (1 + t)
    slope = half + 0.5 * v * (1 - t * t) * 0.7978845608028654 * (1 + 3 * 0.044715 * square)
    return v * half, slope


def dot(a, b):
    return jnp.dot(a, b, preferred_element_type=F32)


def dot_t(a, b):
    return lax.dot_general(a, b, (((1,), (1,)), ((), ())), preferred_element_type=F32)


def t_dot(a, b):
    return lax.dot_general(a, b, (((0,), (0,)), ((), ())), preferred_element_type=F32)


MESH = pl.DeviceIdType.MESH
DMA = pltpu.SemaphoreType.DMA


def shifted(axis, step):
    return lax.rem(lax.axis_index(axis) + step, lax.axis_size(axis))


def greet(peers):
    barrier = pltpu.get_barrier_semaphore()
    for peer in peers:
        pl.semaphore_signal(barrier, inc=1, device_id=peer, device_id_type=MESH)
    pl.semaphore_wait(barrier, len(peers))


def ring(axis):
    return [{axis: shifted(axis, k)} for k in range(1, lax.axis_size(axis))]


def push(src, dst, send, recv, peer):
    copy = pltpu.make_async_remote_copy(
        src_ref=src, dst_ref=dst, send_sem=send, recv_sem=recv, device_id=peer, device_id_type=MESH
    )
    copy.start()
    return copy


def finish(copies):
    for copy in copies:
        copy.wait_recv()


def vmem_call(kernel, name, number, outs, scratch, *args):
    return pl.pallas_call(
        kernel,
        out_shape=outs,
        in_specs=[pl.BlockSpec(memory_space=pltpu.VMEM)] * len(args),
        out_specs=jax.tree.map(lambda _: pl.BlockSpec(memory_space=pltpu.VMEM), outs),
        scratch_shapes=scratch,
        compiler_params=pltpu.CompilerParams(
            collective_id=number, has_side_effects=True, vmem_limit_bytes=56 << 20
        ),
        name=name,
    )(*args)


def gather_tile(feat, band):
    count = lax.axis_size("tile")

    def kernel(feat_ref, band_ref, feats_ref, bands_ref, send, recv):
        me = lax.axis_index("tile")
        peers = ring("tile")
        greet(peers)
        copies = []
        for k, peer in enumerate(peers):
            copies.append(push(feat_ref, feats_ref.at[me], send.at[0, k], recv.at[0, k], peer))
            copies.append(push(band_ref, bands_ref.at[me], send.at[1, k], recv.at[1, k], peer))
        feats_ref[me] = feat_ref[...]
        bands_ref[me] = band_ref[...]
        for copy in copies:
            copy.wait()

    outs = [jax.ShapeDtypeStruct((count,) + a.shape, a.dtype) for a in (feat, band)]
    return vmem_call(kernel, "gather_tile", 0, outs, [DMA((2, count - 1))] * 2, feat, band)


def fold_exchange(fold, part, head):
    T, M = lax.axis_size("tile"), lax.axis_size("mp")

    def kernel(fold_ref, part_ref, head_ref, sum_ref, parts_ref, heads_ref, slots, send, recv, xsend, xrecv):
        me, mine = lax.axis_index("tile"), lax.axis_index("mp")
        tiles, mps = ring("tile"), ring("mp")
        greet(tiles + mps)
        first = []
        for k, peer in enumerate(tiles):
            first.append(push(fold_ref.at[peer["tile"]], slots.at[k], send.at[0, k], recv.at[0, k], peer))
        across = []
        for k, peer in enumerate(mps):
            across.append(push(part_ref, parts_ref.at[mine], xsend.at[0, k], xrecv.at[0, k], peer))
            across.append(push(head_ref, heads_ref.at[mine], xsend.at[1, k], xrecv.at[1, k], peer))
        parts_ref[mine] = part_ref[...]
        heads_ref[mine] = head_ref[...]
        finish(first)
        total = fold_ref[me].astype(F32)
        for k in range(T - 1):
            total = total + slots[k].astype(F32)
        sum_ref[me] = total.astype(BF)
        second = []
        for k, peer in enumerate(tiles):
            second.append(push(sum_ref.at[me], sum_ref.at[me], send.at[1, k], recv.at[1, k], peer))
        finish(second + across)
        for copy in first + second + across:
            copy.wait_send()

    outs = [
        jax.ShapeDtypeStruct(fold.shape, BF),
        jax.ShapeDtypeStruct((M,) + part.shape, BF),
        jax.ShapeDtypeStruct((M,) + head.shape, BF),
    ]
    scratch = [pltpu.VMEM((T - 1,) + fold.shape[1:], BF)] + [DMA((2, T - 1))] * 2 + [DMA((2, M - 1))] * 2
    return vmem_call(kernel, "fold_exchange", 1, outs, scratch, fold, part, head)


def teacher(x64, embed, folded, d_out, headt, target, factor, pixels):
    S, M, T = (lax.axis_size(a) for a in ("segment", "mp", "tile"))
    C, q, R = target.shape
    owners = S * M * T
    group = min(owners, 256 // q)
    rows = group * q
    blocks = owners // group
    K = x64.shape[1]
    dim = embed.shape[1]
    dt = d_out.shape[1]
    slabs, _, slab = folded.shape
    hid = slabs * slab
    step_cols = min(512, dim)
    most = max(S, M, T) - 1

    def kernel(
        x_ref, embed_ref, fold_ref, dout_hbm, head_ref, target_ref, factor_ref, out_ref,
        dout, pre_ref, slope_ref, scale_ref, unit_ref,
        part_ref, grad_ref, s_in, s_sum, m_in, m_sum, t_in, send, recv, load,
    ):
        s, m, t = (lax.axis_index(a) for a in ("segment", "mp", "tile"))
        segs, mps, tiles = ring("segment"), ring("mp"), ring("tile")
        fetch = pltpu.make_async_copy(dout_hbm.at[pl.ds(s * hid, hid)], dout, load)
        fetch.start()
        once = jnp.logical_and(s == 0, m == 0).astype(F32)
        own_cols = pl.ds(pl.multiple_of(t * dt, dt), dt)

        def scales(c, i):
            x = x_ref[c, pl.ds(i * rows, rows), :]
            total = jnp.zeros((rows, 1), F32)
            unit = jnp.zeros((rows, pixels), F32)
            for b in range(dim // step_cols):
                cols = slice(b * step_cols, (b + 1) * step_cols)
                e = dot(x, embed_ref[:, cols]).astype(BF)
                e32 = e.astype(F32)
                total = total + jnp.sum(e32 * e32, axis=1, keepdims=True)
                unit = unit + dot_t(e, embed_ref[:pixels, cols])
            scale = lax.rsqrt(total / dim + 1e-05)
            scale_ref[c, i] = scale
            unit_ref[c, i] = unit * scale

        def forward(c, i):
            scales(c, i)
            x = x_ref[c, pl.ds(i * rows, rows), :]
            scale = scale_ref[c, i]

            def hidden(h, acc):
                pre = scale * dot(x, fold_ref[h])
                act, slope = gelu_and_slope(pre)
                pre_ref[c, i, h] = pre
                slope_ref[c, i, h] = slope
                return acc + dot(act.astype(BF), dout[pl.ds(pl.multiple_of(h * slab, slab), slab), :])

            start = once * dot(x, embed_ref[:, own_cols]).astype(BF).astype(F32)
            acc = lax.fori_loop(0, slabs, hidden, start)
            part = dot_t(acc.astype(BF), head_ref[...]).astype(BF)
            part_ref[c, pl.ds(i * group, group)] = part.reshape(group, q, R)

        def backward(c, i):
            grad = grad_ref[c, pl.ds(i * group, group)].reshape(rows, R)
            gd = dot(grad, head_ref[...]).astype(BF)
            direct = once * dot_t(gd, embed_ref[:pixels, own_cols])

            def hidden(h, carry):
                acc, along = carry
                back = dot_t(gd, dout[pl.ds(pl.multiple_of(h * slab, slab), slab), :])
                gh = slope_ref[c, i, h] * back
                along = along + jnp.sum(gh * pre_ref[c, i, h], axis=1, keepdims=True)
                return acc + dot_t(gh.astype(BF), fold_ref[h, :pixels, :]), along

            acc, along = lax.fori_loop(
                0, slabs, hidden, (jnp.zeros((rows, pixels), F32), jnp.zeros((rows, 1), F32))
            )
            result = scale_ref[c, i] * (acc - unit_ref[c, i] * (along / dim)) + direct
            out_ref[c, pl.ds(i * rows, rows), :] = result.astype(BF)

        def over(function, c):
            if blocks == 1:
                function(c, 0)
            else:
                lax.fori_loop(0, blocks, lambda i, _: (function(c, i), 0)[1], 0)

        live = [None] * C
        everything = []

        def launch(c, stage, peers, source, landing):
            live[c] = [
                push(source(k, p), landing(k), send.at[stage, c, k], recv.at[stage, c, k], p)
                for k, p in enumerate(peers)
            ]
            everything.extend(live[c])

        def advance(c, stage):
            if stage > 0:
                finish(live[c])
            if stage == 0:
                launch(c, 0, segs, lambda k, p: part_ref.at[c, pl.ds(p["segment"] * M * T, M * T)], lambda k: s_in.at[c, k])
            if stage == 1:
                total = part_ref[c, pl.ds(s * M * T, M * T)].astype(F32)
                for k in range(S - 1):
                    total = total + s_in[c, k].astype(F32)
                s_sum[c] = total.astype(BF)
                launch(c, 1, mps, lambda k, p: s_sum.at[c, pl.ds(p["mp"] * T, T)], lambda k: m_in.at[c, k])
            if stage == 2:
                total = s_sum[c, pl.ds(m * T, T)].astype(F32)
                for k in range(M - 1):
                    total = total + m_in[c, k].astype(F32)
                m_sum[c] = total.astype(BF)
                launch(c, 2, tiles, lambda k, p: m_sum.at[c, p["tile"]], lambda k: t_in.at[c, k])
            if stage == 3:
                total = m_sum[c, t].astype(F32)
                for k in range(T - 1):
                    total = total + t_in[c, k].astype(F32)
                grad = factor_ref[c] * (total - target_ref[c].astype(F32))
                place = (s * M + m) * T + t
                grad_ref[c, place] = grad.astype(BF)
                own = grad_ref.at[c, place]
                launch(c, 3, tiles, lambda k, p: own, lambda k: own)
            if stage == 4:
                own = grad_ref.at[c, pl.ds((s * M + m) * T, T)]
                launch(c, 4, mps, lambda k, p: own, lambda k: own)
            if stage == 5:
                own = grad_ref.at[c, pl.ds(s * M * T, M * T)]
                launch(c, 5, segs, lambda k, p: own, lambda k: own)

        greet(segs + mps + tiles)
        fetch.wait()
        for step in range(7 + C):
            for c in range(C):
                stage = step - c - 1
                if 0 <= stage <= 6:
                    advance(c, stage)
            for c in range(C):
                if step == c:
                    over(forward, c)
                if step - c - 1 == 6:
                    over(backward, c)
        for copy in everything:
            copy.wait_send()

    vm = pltpu.VMEM
    scratch = [
        vm((hid, dt), BF),
        vm((C, blocks, slabs, rows, slab), F32),
        vm((C, blocks, slabs, rows, slab), F32),
        vm((C, blocks, rows, 1), F32),
        vm((C, blocks, rows, pixels), F32),
        vm((C, owners, q, R), BF),
        vm((C, owners, q, R), BF),
        vm((C, S - 1, M * T, q, R), BF),
        vm((C, M * T, q, R), BF),
        vm((C, M - 1, T, q, R), BF),
        vm((C, T, q, R), BF),
        vm((C, T - 1, q, R), BF),
        DMA((6, C, most)),
        DMA((6, C, most)),
        DMA,
    ]
    whole = pl.BlockSpec(memory_space=pltpu.VMEM)
    return pl.pallas_call(
        kernel,
        out_shape=jax.ShapeDtypeStruct((C, owners * q, pixels), BF),
        in_specs=[whole] * 3 + [pl.BlockSpec(memory_space=pl.ANY)] + [whole] * 3,
        out_specs=whole,
        scratch_shapes=scratch,
        compiler_params=pltpu.CompilerParams(
            collective_id=2, has_side_effects=True, vmem_limit_bytes=56 << 20
        ),
        name="teacher",
    )(x64.reshape(C, owners * q, K), embed, folded, d_out, headt, target, factor)


def token_sum(part):
    T, rows, width = part.shape
    S, M = lax.axis_size("segment"), lax.axis_size("mp")
    holders = S * M
    most = max(holders, T) - 1

    def kernel(part_ref, sum_ref, t_in, t_sum, h_in, send, recv):
        t = lax.axis_index("tile")
        tiles = ring("tile")
        others = [
            {"segment": shifted("segment", k // M), "mp": shifted("mp", k % M)} for k in range(1, holders)
        ]
        greet(tiles + others)
        everything = []

        def launch(stage, peers, source, landing):
            copies = [
                push(source(p), landing(k), send.at[stage, k], recv.at[stage, k], p)
                for k, p in enumerate(peers)
            ]
            everything.extend(copies)
            finish(copies)

        launch(0, tiles, lambda p: part_ref.at[p["tile"]], lambda k: t_in.at[k])
        total = part_ref[t].astype(F32)
        for k in range(T - 1):
            total = total + t_in[k].astype(F32)
        t_sum[...] = total.astype(BF)
        launch(1, others, lambda p: t_sum, lambda k: h_in.at[k])
        total = t_sum[...].astype(F32)
        for k in range(holders - 1):
            total = total + h_in[k].astype(F32)
        sum_ref[t] = total.astype(BF)
        own = sum_ref.at[t]
        launch(2, tiles, lambda p: own, lambda k: own)
        for copy in everything:
            copy.wait_send()

    scratch = [
        pltpu.VMEM((T - 1, rows, width), BF),
        pltpu.VMEM((rows, width), BF),
        pltpu.VMEM((holders - 1, rows, width), BF),
        DMA((3, most)),
        DMA((3, most)),
    ]
    return vmem_call(kernel, "token_sum", 3, jax.ShapeDtypeStruct(part.shape, BF), scratch, part)


def project_sum(part):
    T, S, M = (lax.axis_size(a) for a in ("tile", "segment", "mp"))
    count = T * M

    def kernel(part_ref, sum_ref, slots, send, recv):
        s, t = lax.axis_index("segment"), lax.axis_index("tile")
        me = t * M + lax.axis_index("mp")
        peers = [
            {"tile": shifted("tile", k // M), "mp": shifted("mp", k % M)} for k in range(1, count)
        ]
        greet(peers)
        copies = []
        for k, peer in enumerate(peers):
            copies.append(
                push(part_ref.at[peer["tile"] * S + s], slots.at[me], send.at[k], recv.at[k], peer)
            )
        slots[me] = part_ref[t * S + s]
        finish(copies)
        total = slots[0]
        for k in range(1, count):
            total = total + slots[k]
        sum_ref[...] = total
        for copy in copies:
            copy.wait_send()

    scratch = [pltpu.VMEM((count,) + part.shape[1:], F32), DMA((count - 1,)), DMA((count - 1,))]
    return vmem_call(kernel, "project_sum", 4, jax.ShapeDtypeStruct(part.shape[1:], F32), scratch, part)


def body(spectra, valid, project, enc_in, enc_out, tok_embed, band_embed, dec_in, dec_out, head):
    tile, seg, mp = (lax.axis_index(a) for a in ("tile", "segment", "mp"))
    T, S, M = (lax.axis_size(a) for a in ("tile", "segment", "mp"))
    batches, per_tile, pixels, bands = spectra.shape
    codes = project.shape[1]
    width = bands // codes
    local = batches * per_tile
    share = local // (S * M)
    parts = 2 if share % 2 == 0 else 1
    piece = share // parts
    rows = T * local
    student = codes * pixels
    dim = tok_embed.shape[1]
    dt = dec_in.shape[0]
    hid = dec_in.shape[1] // S

    patches = spectra.reshape(local, pixels, bands)
    flat = patches.reshape(local * pixels, bands)
    feat_local = (
        dot(flat, project).astype(BF).reshape(local, pixels, codes).transpose(0, 2, 1).reshape(local, student)
    )
    feats, band_all = gather_tile(feat_local, band_embed)
    feats = (
        feats.reshape(T, parts, S, M, piece, student).transpose(1, 2, 3, 0, 4, 5).reshape(rows, student)
    )
    band_all = band_all.reshape(codes, dim)

    embed = jnp.concatenate([tok_embed, band_all], axis=0)
    embed_z = lax.dynamic_slice_in_dim(embed, tile * dt, dt, 1)
    d_in = lax.dynamic_slice_in_dim(dec_in, seg * hid, hid, 1)
    fold_part = dot(embed_z, d_in).astype(BF).reshape(-1, T, hid // T).transpose(1, 0, 2)

    feats32 = feats.astype(F32)
    normed = (feats32 * inv_rms(feats32)).astype(BF)
    pre_act, pre_slope = gelu_and_slope(dot(normed, enc_in))
    act_out = pre_act.astype(BF)
    folded, summed, heads = fold_exchange(fold_part, dot(act_out, enc_out).astype(BF), head.T)
    headt = heads.reshape(-1, dt)
    if hid // T < 128:
        folded = folded.transpose(1, 0, 2).reshape(1, -1, hid)
    summed = jnp.sum(summed.astype(F32), axis=0)
    encoded = (feats32 + summed).astype(BF)

    tokens = rows * codes
    tok = encoded.reshape(tokens, pixels)
    which = jnp.broadcast_to(jnp.eye(codes, dtype=BF), (rows, codes, codes)).reshape(tokens, codes)
    x64 = jnp.concatenate([tok, which], axis=1)
    place = (seg * M + mp) * piece

    def mine(a):
        a = a.reshape((parts, S * M * piece) + a.shape[1:])
        a = lax.dynamic_slice_in_dim(a, place, piece, 1)
        return a.reshape((share,) + a.shape[2:])

    own_patches = mine(patches)
    target = (
        own_patches.reshape(share, pixels, codes, width).transpose(0, 2, 1, 3).reshape(share * codes, -1)
    )
    total_valid = jnp.sum(valid.astype(F32))
    loss_scale = 2.0 * batches * valid.shape[1] / total_valid
    own_valid = lax.dynamic_slice_in_dim(valid, tile * per_tile, per_tile, 1).reshape(local)
    own_valid = mine(own_valid)
    column = jnp.arange(pixels * width, dtype=jnp.int32) // width
    mask = (column[None, :] < jnp.repeat(own_valid, codes)[:, None]).astype(F32)
    block = (parts, piece * codes, pixels * width)
    grad_tok = teacher(
        x64,
        embed,
        folded,
        dec_out,
        headt,
        target.reshape(block),
        (loss_scale * mask).reshape(block),
        pixels,
    )
    grad_encoded = token_sum(grad_tok.reshape(T, local, student)).reshape(rows, student)

    grad_act = (pre_slope * dot_t(grad_encoded, enc_out)).astype(BF)
    columns = student // (T * S)
    start = (tile * S + seg) * columns
    grad_out = t_dot(act_out, lax.dynamic_slice_in_dim(grad_encoded, start, columns, 1))
    grad_in = t_dot(lax.dynamic_slice_in_dim(normed, start, columns, 1), grad_act)
    own_rows = lambda a: lax.dynamic_slice_in_dim(
        a.reshape(parts * S * M, T, piece, student), tile, 1, 1
    ).reshape(local, student)
    grad_normed = own_rows(dot_t(grad_act, enc_in).astype(BF)).astype(F32)
    grad_feat = (
        jnp.where(mp == 0, own_rows(grad_encoded).astype(F32), 0.0)
        + rms_back(feat_local.astype(F32), grad_normed)
    ).astype(BF)
    grad_codes = grad_feat.reshape(local, codes, pixels).transpose(0, 2, 1).reshape(-1, codes)
    grad_proj = project_sum(t_dot(flat, grad_codes).reshape(T * S, -1, codes))
    return (grad_proj, grad_in, grad_out)


def solution(mesh):
    placed = (
        P(None, ("groups", "tile"), None, None),
        P(None, "groups"),
        P(),
        P(None, "mp"),
        P("mp", None),
        P(),
        P("tile", None),
        P("tile", "mp"),
        P("mp", "tile"),
        P("tile", "mp"),
    )
    return jax.shard_map(
        body,
        mesh=mesh,
        in_specs=placed,
        out_specs=(
            P(("groups", "tile", "segment"), None),
            P(("groups", "tile", "segment"), "mp"),
            P(("groups", "mp"), ("tile", "segment")),
        ),
        check_vma=False,
    )
```
